32 devices in a mesh: groups: 2 (over y), patch: 4 (over z), feat: 2 (over x), sub: 2 (over core).
Axes of the slice: x: 2, y: 2, z: 4, core: 2. Of those that a mesh axis runs over, the one named last changes fastest.
Arguments:
- grid_feat: bfloat16 [32768, 512], P(('groups', 'patch', 'feat', 'sub')), parts along dimension 0, may hold values from -6 to 6
- block_owner: int32 [256], P(('groups', 'patch', 'feat', 'sub')), parts along dimension 0, may hold values from 0 to 3, as said below
- enc_node: int32 [32768], P(('groups', 'patch', 'feat', 'sub')), parts along dimension 0, may hold values from 0 to 31
- dec_node: int32 [32768], P(('groups', 'patch', 'feat', 'sub')), parts along dimension 0, may hold values from 0 to 31
- mesh_feat: bfloat16 [1024, 512], P(('groups', 'patch', 'feat', 'sub')), parts along dimension 0, may hold values from -6 to 6
- edge_feat: bfloat16 [8192, 512], P(('groups', 'patch', 'feat', 'sub')), parts along dimension 0, may hold values from -6 to 6
- senders: int32 [8192], P(('groups', 'patch', 'feat', 'sub')), parts along dimension 0, may hold values from 0 to 191
- receivers: int32 [8192], P(('groups', 'patch', 'feat', 'sub')), parts along dimension 0, may hold values from 0 to 31
- enc_w1: bfloat16 [512, 512], P(('feat', 'sub')), may hold values from -0.25 to 0.25
- enc_w2: bfloat16 [512, 512], P(('feat', 'sub')), may hold values from -0.25 to 0.25
- gn_w1: bfloat16 [1024, 512], P(('feat', 'sub')), may hold values from -0.1875 to 0.1875
- gn_w2: bfloat16 [512, 512], P(('feat', 'sub')), may hold values from -0.25 to 0.25
- edge_w1: bfloat16 [1536, 512], P(('feat', 'sub')), may hold values from -0.15625 to 0.15625
- edge_w2: bfloat16 [512, 512], P(('feat', 'sub')), may hold values from -0.25 to 0.25
- node_w1: bfloat16 [1024, 512], P(('feat', 'sub')), may hold values from -0.1875 to 0.1875
- node_w2: bfloat16 [512, 512], P(('feat', 'sub')), may hold values from -0.25 to 0.25
- dec_w1: bfloat16 [1024, 512], P(('feat', 'sub')), may hold values from -0.1875 to 0.1875
- dec_w2: bfloat16 [512, 512], P(('feat', 'sub')), may hold values from -0.25 to 0.25
Outputs:
- grid_out: bfloat16 [32768, 512], P(('groups', 'patch', 'feat', 'sub')), parts along dimension 0
The draws below stay inside these ranges and needn't reach their ends.
There are 2 independent parts, one for each index of `groups`. The reference program is written for one: setup_inputs(seed, part) draws one part's arguments, and reference() takes and returns one part's arrays. A program takes and returns all parts, laid end to end along the dimension named above; an argument that names none is the same for every part. Nothing has to cross between parts.
Inputs may be any that keep to these rules, and one draw needn't show every extreme that they name: `block_owner`: among the 8 blocks of one device along patch+feat+sub (aligned runs of 8 entries), at most 2 name the same patch, and one patch is named by exactly 2 blocks of every device.
All inputs are finite; a program needn't handle non-finite values.
Results may differ from the reference program's by a relative error of at most 0.015.
Values may be sent and summed in bfloat16 or wider, within the bound.
A program may use at most 64 MiB of HBM per device.

```python
import jax
import jax.numpy as jnp
from jax import lax

D = 512
H = 512
ROWS_BLK = 128
BLK_DEV = 8
MNODE_DEV = 32
EDGE_DEV = 256
BND = 32
LANES = 4
CAP = 2
PATCH_NODES = 128
MESH = 512
GRID = 16384
NBLK = 128
EDGES = 4096
N_PATCH = 4


def draw_block_owner(key, part):
    key = jax.random.fold_in(key, 11)
    device_count = NBLK // BLK_DEV
    favoured = jax.random.randint(jax.random.fold_in(key, 1), (), 0, N_PATCH).astype(jnp.int32)
    slot_owner = (jnp.arange(N_PATCH * CAP, dtype=jnp.int32) // CAP + favoured) % N_PATCH

    def one_device(device_key):
        first_key, second_key = jax.random.split(device_key)
        others = jax.random.permutation(first_key, slot_owner[CAP:])
        chosen = jnp.concatenate([slot_owner[:CAP], others[:BLK_DEV - CAP]])
        return jax.random.permutation(second_key, chosen)
    device_keys = jax.random.split(jax.random.fold_in(key, 2), device_count)
    return jax.vmap(one_device)(device_keys).reshape(-1).astype(jnp.int32)


def touch_ends(values, stream_key, low, largest):
    shape = values.shape
    place = [jax.random.randint(jax.random.fold_in(stream_key, axis), (), 0, shape[axis]) for axis in range(len(shape))]
    values = values.at[tuple(place)].set(low)
    longest = shape.index(max(shape))
    place[longest] = (place[longest] + 1) % shape[longest]
    return values.at[tuple(place)].set(largest)


def block_scale(stream_key, extent, cuts, least, top_value):
    factor_of = 1.0
    for dim, blocks in cuts:
        draws = jax.random.uniform(jax.random.fold_in(jax.random.fold_in(stream_key, 6), dim), (blocks,), jnp.float32, least / len(cuts), top_value / len(cuts))
        factor_of = factor_of * jnp.repeat(jnp.exp(draws), extent[dim] // blocks).reshape((-1,) + (1,) * (len(extent) - 1 - dim))
    return factor_of


def gaussian(rng, shape, width, most, shards=(), kind=jnp.bfloat16):
    factor_of = block_scale(rng, shape, shards, -0.22, 0.18) if shards else 1.0
    result = jax.random.normal(rng, shape, jnp.float32) * width * factor_of
    return jnp.minimum(jnp.maximum(result, -most), most).astype(kind)


def setup_inputs(seed: int = 0, part: int = 0) -> dict:
    seeds = jax.random.split(jax.random.key(seed), 19)
    part_keys = jax.random.split(jax.random.fold_in(seeds[18], part), 19)
    return {
        "grid_feat": gaussian(part_keys[0], (GRID, D), 1.0, 6.0, ((0, 16),)),
        "block_owner": draw_block_owner(jax.random.fold_in(jax.random.fold_in(seeds[18], part), 71), part),
        "enc_node": touch_ends(jax.random.randint(part_keys[2], (GRID,), 0, MNODE_DEV), jax.random.fold_in(part_keys[2], 1), 0, MNODE_DEV - 1).astype(jnp.int32),
        "dec_node": touch_ends(jax.random.randint(part_keys[3], (GRID,), 0, MNODE_DEV), jax.random.fold_in(part_keys[3], 1), 0, MNODE_DEV - 1).astype(jnp.int32),
        "mesh_feat": gaussian(part_keys[4], (MESH, D), 1.0, 6.0, ((0, 16),)),
        "edge_feat": gaussian(part_keys[5], (EDGES, D), 1.0, 6.0, ((0, 16),)),
        "senders": touch_ends(jax.random.randint(part_keys[6], (EDGES,), 0, PATCH_NODES + 2 * BND), jax.random.fold_in(part_keys[6], 1), 0, (PATCH_NODES + 2 * BND) - 1).astype(jnp.int32),
        "receivers": touch_ends(jax.random.randint(part_keys[7], (EDGES,), 0, MNODE_DEV), jax.random.fold_in(part_keys[7], 1), 0, MNODE_DEV - 1).astype(jnp.int32),
        "enc_w1": gaussian(seeds[8], (D, H), D ** -0.5, 0.25, ((0, 4),)),
        "enc_w2": gaussian(seeds[9], (H, D), H ** -0.5, 0.25, ((0, 4),)),
        "gn_w1": gaussian(seeds[10], (2 * D, H), (2 * D) ** -0.5, 0.1875, ((0, 4),)),
        "gn_w2": gaussian(seeds[11], (H, D), H ** -0.5, 0.25, ((0, 4),)),
        "edge_w1": gaussian(seeds[12], (3 * D, H), (3 * D) ** -0.5, 0.15625, ((0, 4),)),
        "edge_w2": gaussian(seeds[13], (H, D), H ** -0.5, 0.25, ((0, 4),)),
        "node_w1": gaussian(seeds[14], (2 * D, H), (2 * D) ** -0.5, 0.1875, ((0, 4),)),
        "node_w2": gaussian(seeds[15], (H, D), H ** -0.5, 0.25, ((0, 4),)),
        "dec_w1": gaussian(seeds[16], (2 * D, H), (2 * D) ** -0.5, 0.1875, ((0, 4),)),
        "dec_w2": gaussian(seeds[17], (H, D), H ** -0.5, 0.25, ((0, 4),)),
    }


def layer_norm(values):
    centred = values - lax.optimization_barrier(jnp.mean(values, axis=-1, keepdims=True))
    spread = lax.optimization_barrier(jnp.mean(centred * centred, axis=-1, keepdims=True))
    return centred * lax.rsqrt(spread + 1e-05)

def network(inputs, first, second):
    hidden = jax.nn.silu(jnp.dot(inputs, first, preferred_element_type=jnp.float32)).astype(jnp.bfloat16)
    return layer_norm(jnp.dot(hidden, second, preferred_element_type=jnp.float32))

def reference(grid_feat, block_owner, enc_node, dec_node, mesh_feat, edge_feat, senders, receivers, enc_w1, enc_w2, gn_w1, gn_w2, edge_w1, edge_w2, node_w1, node_w2, dec_w1, dec_w2):
    row_dev = BLK_DEV * ROWS_BLK
    device_count = N_PATCH * LANES
    lane_of_row = jnp.arange(GRID, dtype=jnp.int32) // row_dev % LANES
    owner_row = jnp.repeat(block_owner, ROWS_BLK).astype(jnp.int32)
    base_node = (owner_row * LANES + lane_of_row) * MNODE_DEV
    enc_target = (base_node + enc_node).astype(jnp.int32)
    dec_source = (base_node + dec_node).astype(jnp.int32)
    grid_blocks = grid_feat.reshape(device_count, row_dev, D)

    def encode(block):
        return network(block, enc_w1, enc_w2).astype(jnp.bfloat16)
    messages = lax.map(encode, grid_blocks).reshape(GRID, D)
    gathered = jax.ops.segment_sum(messages.astype(jnp.float32), enc_target, num_segments=MESH)
    gathered_half = gathered.astype(jnp.bfloat16)
    mesh_mid = (mesh_feat + network(jnp.concatenate([mesh_feat, gathered_half], 1), gn_w1, gn_w2)).astype(jnp.bfloat16)
    edge_dev = jnp.arange(EDGES, dtype=jnp.int32) // EDGE_DEV
    edge_patch = edge_dev // LANES
    sender_node = ((edge_patch * PATCH_NODES + senders - BND) % MESH).astype(jnp.int32)
    receiver_node = (edge_dev * MNODE_DEV + receivers).astype(jnp.int32)
    edge_inputs = jnp.concatenate([edge_feat, mesh_mid[sender_node], mesh_mid[receiver_node]], 1)
    edge_new = (edge_feat + network(edge_inputs, edge_w1, edge_w2)).astype(jnp.bfloat16)
    edge_sum = jax.ops.segment_sum(edge_new.astype(jnp.float32), receiver_node, num_segments=MESH).astype(jnp.bfloat16)
    mesh_out = (mesh_mid + network(jnp.concatenate([mesh_mid, edge_sum], 1), node_w1, node_w2)).astype(jnp.bfloat16)

    def decode(pair):
        block, source = pair
        inputs = jnp.concatenate([block, mesh_out[source]], 1)
        return (block + network(inputs, dec_w1, dec_w2)).astype(jnp.bfloat16)
    decoded = lax.map(decode, (grid_blocks, dec_source.reshape(device_count, row_dev)))
    return decoded.reshape(GRID, D)
```

```python
import functools

import jax
import jax.numpy as jnp
from jax import lax
from jax.experimental import pallas as pl
from jax.experimental.pallas import tpu as pltpu
from jax.sharding import PartitionSpec as P

MESH = pl.DeviceIdType.MESH
BF = jnp.bfloat16
F32 = jnp.float32


def dot(a, b):
    return jnp.dot(a, b, preferred_element_type=F32)


def dot_t(a, b):
    return lax.dot_general(a, b, (((0,), (0,)), ((), ())), preferred_element_type=F32)


def silu(u):
    half = 0.5 * u
    return (half + half * jnp.tanh(half)).astype(BF)


def layer_norm(values):
    centred = values - jnp.mean(values, axis=-1, keepdims=True)
    spread = jnp.mean(centred * centred, axis=-1, keepdims=True)
    return centred * lax.rsqrt(spread + 1e-05)


def kernel(sizes, *refs):
    G, NP, F, S = sizes
    L = F * S
    grid_h, owner, enc_node, dec_node, mesh, edge_h, senders, receivers = refs[:8]
    shards = refs[8:18]
    out_h = refs[18]
    full = refs[19:29]
    (
        grid, edge, msgs, outs, part, part_in, ext, lane_p,
        loc_sem, own_sem, w_send, w_recv, p_send, p_recv, m_send, n_send, m_recv, o_send, o_recv, out_sem,
    ) = refs[29:]
    g, p, f, s = (lax.axis_index(a) for a in ("groups", "patch", "feat", "sub"))
    lane = f * S + s
    n_w = len(shards)
    rows, width = grid.shape
    nodes = mesh.shape[0]
    n_edges = edge.shape[0]
    blocks = owner.shape[0]
    blk = rows // blocks
    chunk = 2 * blk
    n_chunks = rows // chunk
    sent = []

    def turn(i, d, n):
        return lax.rem(i + d, n)

    def send(src, dst, ssem, rsem, dev):
        c = pltpu.make_async_remote_copy(
            src_ref=src, dst_ref=dst, send_sem=ssem, recv_sem=rsem, device_id=dev, device_id_type=MESH
        )
        c.start()
        sent.append(c)

    def got(dst, sem):
        pltpu.make_async_copy(dst, dst, sem).wait()

    local = [pltpu.make_async_copy(grid_h, grid, loc_sem.at[0]), pltpu.make_async_copy(edge_h, edge, loc_sem.at[1])]
    for c in local:
        c.start()

    def rows_of(i, ln, h=None):
        r = shards[i].shape[0]
        if h is None:
            return full[i].at[pl.ds(pl.multiple_of(ln * r, 16), r)]
        return full[i].at[pl.ds(pl.multiple_of(ln * r + h * (r // G), 16), r // G)]

    own = [pltpu.make_async_copy(shards[i], rows_of(i, lane), own_sem.at[i]) for i in range(n_w)]
    for c in own:
        c.start()

    barrier = pltpu.get_barrier_semaphore()
    partners = [(turn(g, d, G), p, f, s) for d in range(1, G)]
    partners += [(g, turn(p, d, NP), f, s) for d in range(1, NP)]
    partners += [(g, p, turn(f, df, F), turn(s, ds, S)) for df in range(F) for ds in range(S) if df or ds]
    near = sorted({1 % NP, (NP - 1) % NP} - {0})
    partners += [
        (g, turn(p, d, NP), turn(f, df, F), turn(s, ds, S))
        for d in near for df in range(F) for ds in range(S) if df or ds
    ]
    for dev in partners:
        pl.semaphore_signal(barrier, inc=1, device_id=dev, device_id_type=MESH)
    pl.semaphore_wait(barrier, len(partners))

    slot = [0] * n_w

    def w_out(i, src, dst, rsem, dev):
        send(src, dst, w_send.at[i, slot[i]], rsem, dev)
        slot[i] += 1

    def hop_a(i):
        r = shards[i].shape[0] // G
        for df in range(1, F):
            src = shards[i].at[pl.ds(pl.multiple_of(g * r, 16), r)]
            w_out(i, src, rows_of(i, lane, g), w_recv.at[i, lane, g], (g, p, turn(f, df, F), s))
        for ds in range(1, S):
            w_out(i, shards[i], rows_of(i, lane), w_recv.at[i, lane, 0], (g, p, f, turn(s, ds, S)))

    def hop_b(i):
        for df in range(1, F):
            ln = turn(f, df, F) * S + s
            buf, sem = rows_of(i, ln, g), w_recv.at[i, ln, g]
            got(buf, sem)
            for dg in range(1, G):
                w_out(i, buf, buf, sem, (turn(g, dg, G), p, f, s))
            for ds in range(1, S):
                w_out(i, buf, buf, sem, (g, p, f, turn(s, ds, S)))

    def hop_c(i):
        for df in range(1, F):
            ln = turn(f, df, F) * S + s
            for dg in range(1, G):
                h = turn(g, dg, G)
                buf, sem = rows_of(i, ln, h), w_recv.at[i, ln, h]
                got(buf, sem)
                for ds in range(1, S):
                    w_out(i, buf, buf, sem, (g, p, f, turn(s, ds, S)))

    def hop_d(i):
        own[i].wait()
        for ds in range(1, S):
            so = turn(s, ds, S)
            got(rows_of(i, f * S + so), w_recv.at[i, f * S + so, 0])
            for df in range(1, F):
                ln = turn(f, df, F) * S + so
                for h in range(G):
                    got(rows_of(i, ln, h), w_recv.at[i, ln, h])

    for i in range(n_w):
        hop_a(i)
    hop_b(0)
    hop_b(1)
    hop_c(0)
    hop_c(1)
    hop_b(2)
    hop_d(0)
    hop_d(1)
    local[0].wait()

    between = {0: [lambda: hop_b(3)], 1: [lambda: hop_c(2)], 2: [lambda: hop_c(3)], 3: []}
    for c in range(n_chunks):
        at = pl.ds(c * chunk, chunk)
        h = silu(dot(grid[at, :], full[0][...]))
        msgs[at, :] = layer_norm(dot(h, full[1][...])).astype(BF)
        for step in between.get(c, []):
            step()

    def one_hot(count, first, row):
        ids = lax.broadcasted_iota(jnp.int32, (count, row.shape[1]), 0) + first
        return jnp.where(ids == row, 1.0, 0.0).astype(BF)

    enc_row = jnp.concatenate(
        [enc_node[:, b * blk:(b + 1) * blk] + owner[b] * nodes for b in range(blocks)], axis=1
    )
    dec_row = jnp.concatenate(
        [dec_node[:, b * blk:(b + 1) * blk] + owner[b] * nodes for b in range(blocks)], axis=1
    )
    some = min(NP, 4)
    for q in range(0, NP, some):
        total = dot(one_hot(some * nodes, q * nodes, enc_row), msgs[...])
        part[q * nodes:(q + some) * nodes, :] = total.astype(BF)

    def node_rows(ref, i):
        return ref.at[pl.ds(pl.multiple_of(i * nodes, 16), nodes)]

    for d in range(1, NP):
        q = turn(p, d, NP)
        send(node_rows(part, q), node_rows(part_in, p), p_send.at[d], p_recv.at[p], (g, q, f, s))
    hop_b(4)
    hop_d(2)
    hop_d(3)
    total = part[pl.ds(pl.multiple_of(p * nodes, 16), nodes), :].astype(F32)
    mesh_v = mesh[...]
    u = dot(mesh_v, full[2][:width, :])
    for d in range(1, NP):
        q = turn(p, d, NP)
        got(node_rows(part_in, q), p_recv.at[q])
        total = total + part_in[pl.ds(pl.multiple_of(q * nodes, 16), nodes), :].astype(F32)
    u = u + dot(total.astype(BF), full[2][width:, :])
    mid = (mesh_v.astype(F32) + layer_norm(dot(silu(u), full[3][...]))).astype(BF)
    mine = pl.multiple_of((lane + 1) * nodes, 16)
    ext[pl.ds(mine, nodes), :] = mid
    src = node_rows(ext, lane + 1)
    k = 0
    for df in range(F):
        for ds in range(S):
            if df or ds:
                send(src, src, m_send.at[k], m_recv.at[lane + 1], (g, p, turn(f, df, F), turn(s, ds, S)))
            k += 1

    edge_ends = []
    for want, d, place in ((L - 1, 1, 0), (0, NP - 1, L + 1)):
        copies = []
        k = 0
        for df in range(F):
            for ds in range(S):
                copies.append(
                    pltpu.make_async_remote_copy(
                        src_ref=src, dst_ref=node_rows(ext, place),
                        send_sem=n_send.at[min(place, 1), k], recv_sem=m_recv.at[place],
                        device_id=(g, turn(p, d, NP), df, ds), device_id_type=MESH,
                    )
                )
                k += 1
        edge_ends.append((want, copies))

        @pl.when(lane == want)
        def _():
            for c in copies:
                c.start()

    hop_b(5)
    hop_c(4)
    hop_c(5)
    hop_b(6)
    hop_d(4)
    hop_d(5)
    local[1].wait()
    edge_v = edge[...]
    recv_row = receivers[...]
    recv_hot = one_hot(nodes, 0, recv_row)
    u = dot(edge_v, full[4][:width, :])
    u = u + dot(dot_t(recv_hot, mid).astype(BF), full[4][2 * width:, :])
    for i in range(L + 2):
        @pl.when(lane + 1 != i)
        def _():
            got(node_rows(ext, i), m_recv.at[i])
    hop_b(7)
    send_hot = one_hot((L + 2) * nodes, 0, senders[...])
    u = u + dot(dot_t(send_hot, ext[...]).astype(BF), full[4][width:2 * width, :])
    edge_new = (edge_v.astype(F32) + layer_norm(dot(silu(u), full[5][...]))).astype(BF)
    edge_sum = dot(recv_hot, edge_new).astype(BF)
    hop_c(6)
    hop_c(7)
    hop_b(8)
    hop_d(6)
    hop_d(7)
    u = dot(mid, full[6][:width, :]) + dot(edge_sum, full[6][width:, :])
    mesh_out = (mid.astype(F32) + layer_norm(dot(silu(u), full[7][...]))).astype(BF)
    hop_b(9)
    hop_c(8)
    hop_c(9)
    hop_d(8)
    lane_p[pl.ds(pl.multiple_of(p * nodes, 16), nodes), :] = dot(mesh_out, full[8][width:, :]).astype(BF)
    for d in range(1, NP):
        send(node_rows(lane_p, p), node_rows(lane_p, p), o_send.at[d], o_recv.at[p], (g, turn(p, d, NP), f, s))
    hop_d(9)
    for d in range(1, NP):
        q = turn(p, d, NP)
        got(node_rows(lane_p, q), o_recv.at[q])

    leave = []
    for c in range(n_chunks):
        at = pl.ds(c * chunk, chunk)
        hot = one_hot(NP * nodes, 0, dec_row[:, c * chunk:(c + 1) * chunk])
        u = dot(grid[at, :], full[8][:width, :]) + dot_t(hot, lane_p[...])
        res = grid[at, :].astype(F32) + layer_norm(dot(silu(u), full[9][...]))
        outs[at, :] = res.astype(BF)
        copy = pltpu.make_async_copy(outs.at[at], out_h.at[at], out_sem.at[c])
        copy.start()
        leave.append(copy)

    for c in sent:
        c.wait_send()
    for want, copies in edge_ends:
        @pl.when(lane == want)
        def _():
            for c in copies:
                c.wait_send()
    for c in leave:
        c.wait()


def per_device(
    sizes, grid_feat, block_owner, enc_node, dec_node, mesh_feat, edge_feat, senders, receivers, *weights
):
    G, NP, F, S = sizes
    L = F * S
    rows, width = grid_feat.shape
    nodes = mesh_feat.shape[0]
    n_edges = edge_feat.shape[0]
    n_w = len(weights)
    any_spec = pl.BlockSpec(memory_space=pl.ANY)
    vmem = pl.BlockSpec(memory_space=pltpu.VMEM)
    smem = pl.BlockSpec(memory_space=pltpu.SMEM)
    dma = pltpu.SemaphoreType.DMA
    hops = (S - 1) + (F - 1) * (1 + (G - 1) + (S - 1) + (G - 1) * (S - 1))
    n_chunks = block_owner.shape[0] // 2
    scratch = [pltpu.VMEM((w.shape[0] * L, w.shape[1]), BF) for w in weights] + [
        pltpu.VMEM((rows, width), BF),
        pltpu.VMEM((n_edges, width), BF),
        pltpu.VMEM((rows, width), BF),
        pltpu.VMEM((rows, width), BF),
        pltpu.VMEM((NP * nodes, width), BF),
        pltpu.VMEM((NP * nodes, width), BF),
        pltpu.VMEM(((L + 2) * nodes, width), BF),
        pltpu.VMEM((NP * nodes, width), BF),
        dma((2,)),
        dma((n_w,)),
        dma((n_w, hops)),
        dma((n_w, L, G)),
        dma((NP,)),
        dma((NP,)),
        dma((L,)),
        dma((2, L)),
        dma((L + 2,)),
        dma((NP,)),
        dma((NP,)),
        dma((n_chunks,)),
    ]
    return pl.pallas_call(
        functools.partial(kernel, sizes),
        out_shape=jax.ShapeDtypeStruct((rows, width), BF),
        in_specs=[any_spec, smem, vmem, vmem, vmem, any_spec, vmem, vmem] + [any_spec] * n_w,
        out_specs=any_spec,
        scratch_shapes=scratch,
        compiler_params=pltpu.CompilerParams(
            collective_id=0, has_side_effects=True, vmem_limit_bytes=56 * 1024 * 1024
        ),
    )(
        grid_feat, block_owner, enc_node.reshape(1, -1), dec_node.reshape(1, -1), mesh_feat, edge_feat,
        senders.reshape(1, -1), receivers.reshape(1, -1), *weights
    )


def solution(mesh):
    every = ("groups", "patch", "feat", "sub")
    sizes = tuple(mesh.shape[a] for a in every)
    row, vec, weight = P(every, None), P(every), P(("feat", "sub"), None)
    in_specs = (row, vec, vec, vec, row, row, vec, vec) + (weight,) * 10
    return jax.shard_map(
        functools.partial(per_device, sizes), mesh=mesh, in_specs=in_specs, out_specs=row, check_vma=False
    )
```

```python
import functools

import jax
import jax.numpy as jnp
from jax import lax
from jax.experimental import pallas as pl
from jax.experimental.pallas import tpu as pltpu
from jax.sharding import PartitionSpec as P

MESH = pl.DeviceIdType.MESH
BF = jnp.bfloat16
F32 = jnp.float32


def dot(a, b):
    return jnp.dot(a, b, preferred_element_type=F32)


def dot_t(a, b):
    return lax.dot_general(a, b, (((0,), (0,)), ((), ())), preferred_element_type=F32)


def silu(u):
    half = 0.5 * u
    return (half + half * jnp.tanh(half)).astype(BF)


def layer_norm(values):
    centred = values - jnp.mean(values, axis=-1, keepdims=True)
    spread = jnp.mean(centred * centred, axis=-1, keepdims=True)
    return centred * lax.rsqrt(spread + 1e-05)


def kernel(sizes, *refs):
    G, NP, F, S = sizes
    L = F * S
    grid_h, owner, enc_node, dec_node, mesh, edge_h, senders, receivers = refs[:8]
    shards = refs[8:18]
    out_h = refs[18]
    full = refs[19:29]
    (
        grid, edge, msgs, outs, ahead, part, part_in, ext, lane_p,
        loc_sem, own_sem, w_send, w_recv, p_send, p_recv, m_send, n_send, m_recv, o_send, o_recv, out_sem, relay_sem,
    ) = refs[29:]
    g, p, f, s = (lax.axis_index(a) for a in ("groups", "patch", "feat", "sub"))
    lane = f * S + s
    n_w = len(shards)
    rows, width = grid.shape
    nodes = mesh.shape[0]
    n_edges = edge.shape[0]
    blocks = owner.shape[0]
    blk = rows // blocks
    chunk = 2 * blk
    n_chunks = rows // chunk
    sent = []

    def turn(i, d, n):
        return lax.rem(i + d, n)

    def send(src, dst, ssem, rsem, dev):
        c = pltpu.make_async_remote_copy(
            src_ref=src, dst_ref=dst, send_sem=ssem, recv_sem=rsem, device_id=dev, device_id_type=MESH
        )
        c.start()
        sent.append(c)

    def got(dst, sem):
        pltpu.make_async_copy(dst, dst, sem).wait()

    local = [pltpu.make_async_copy(grid_h, grid, loc_sem.at[0]), pltpu.make_async_copy(edge_h, edge, loc_sem.at[1])]
    for c in local:
        c.start()

    pairs = ([(g, (1 - g, p, f, s))] if G == 2 else []) + (
        [(lax.rem(p, 2), (g, p + 1 - 2 * lax.rem(p, 2), f, s))] if NP % 2 == 0 else []
    )
    cuts = 2 if pairs else 1

    def half_of(i):
        return pairs[i % len(pairs)][0] if pairs else 0

    def rows_of(i, ln, h=None):
        r = shards[i].shape[0]
        if h is None:
            return full[i].at[pl.ds(pl.multiple_of(ln * r, 16), r)]
        return full[i].at[pl.ds(pl.multiple_of(ln * r + h * (r // cuts), 16), r // cuts)]

    own = [pltpu.make_async_copy(shards[i], rows_of(i, lane), own_sem.at[i]) for i in range(n_w)]
    for c in own:
        c.start()

    barrier = pltpu.get_barrier_semaphore()
    near = [(turn(g, d, G), p, f, s) for d in range(1, G)]
    near += [(g, p, turn(f, df, F), turn(s, ds, S)) for df in range(F) for ds in range(S) if df or ds]
    line = ((p < NP - 1, (g, lax.min(p + 1, NP - 1), f, s)), (p > 0, (g, lax.max(p - 1, 0), f, s)))
    for dev in near:
        pl.semaphore_signal(barrier, inc=1, device_id=dev, device_id_type=MESH)
    for there, dev in line:
        @pl.when(there)
        def _():
            pl.semaphore_signal(barrier, inc=1, device_id=dev, device_id_type=MESH)
    pl.semaphore_wait(barrier, len(near) + sum(there.astype(jnp.int32) for there, _ in line))

    def relay():
        for k in range(2):
            (there, dev), (back, _) = line[k], line[1 - k]

            @pl.when(back)
            def _():
                pl.semaphore_wait(relay_sem.at[k], 1)

            @pl.when(there)
            def _():
                pl.semaphore_signal(relay_sem.at[k], inc=1, device_id=dev, device_id_type=MESH)

    slot = [0] * n_w

    def w_out(i, src, dst, rsem, dev):
        send(src, dst, w_send.at[i, slot[i]], rsem, dev)
        slot[i] += 1

    def hop_a(i):
        r = shards[i].shape[0] // cuts
        h = half_of(i)
        for df in range(1, F):
            src = shards[i].at[pl.ds(pl.multiple_of(h * r, 16), r)]
            w_out(i, src, rows_of(i, lane, h), w_recv.at[i, lane, h], (g, p, turn(f, df, F), s))
        for ds in range(1, S):
            w_out(i, shards[i], rows_of(i, lane), w_recv.at[i, lane, 0], (g, p, f, turn(s, ds, S)))

    def hop_b(i):
        h = half_of(i)
        for df in range(1, F):
            ln = turn(f, df, F) * S + s
            buf, sem = rows_of(i, ln, h), w_recv.at[i, ln, h]
            got(buf, sem)
            if pairs:
                w_out(i, buf, buf, sem, pairs[i % len(pairs)][1])
            for ds in range(1, S):
                w_out(i, buf, buf, sem, (g, p, f, turn(s, ds, S)))

    def hop_c(i):
        if not pairs:
            return
        h = 1 - half_of(i)
        for df in range(1, F):
            ln = turn(f, df, F) * S + s
            buf, sem = rows_of(i, ln, h), w_recv.at[i, ln, h]
            got(buf, sem)
            for ds in range(1, S):
                w_out(i, buf, buf, sem, (g, p, f, turn(s, ds, S)))

    def hop_d(i):
        own[i].wait()
        for ds in range(1, S):
            so = turn(s, ds, S)
            got(rows_of(i, f * S + so), w_recv.at[i, f * S + so, 0])
            for df in range(1, F):
                ln = turn(f, df, F) * S + so
                for h in range(cuts):
                    got(rows_of(i, ln, h), w_recv.at[i, ln, h])

    for i in range(n_w):
        hop_a(i)
    relay()
    hop_b(0)
    hop_b(1)
    hop_c(0)
    hop_b(2)
    hop_c(1)
    hop_d(0)
    hop_d(1)
    local[0].wait()

    between = {n_chunks // 2 - 1: [lambda: hop_b(3), lambda: hop_c(2)], n_chunks - 1: [lambda: hop_c(3)]}
    for c in range(n_chunks):
        at = pl.ds(c * chunk, chunk)
        h = silu(dot(grid[at, :], full[0][...]))
        msgs[at, :] = layer_norm(dot(h, full[1][...])).astype(BF)
        for step in between.get(c, []):
            step()

    def one_hot(count, first, row):
        ids = lax.broadcasted_iota(jnp.int32, (count, row.shape[1]), 0) + first
        return jnp.where(ids == row, 1.0, 0.0).astype(BF)

    enc_row = jnp.concatenate(
        [enc_node[:, b * blk:(b + 1) * blk] + owner[b] * nodes for b in range(blocks)], axis=1
    )
    dec_row = jnp.concatenate(
        [dec_node[:, b * blk:(b + 1) * blk] + owner[b] * nodes for b in range(blocks)], axis=1
    )
    some = min(NP, 4)
    for q in range(0, NP, some):
        total = dot(one_hot(some * nodes, q * nodes, enc_row), msgs[...])
        part[q * nodes:(q + some) * nodes, :] = total.astype(BF)

    def node_rows(ref, i):
        return ref.at[pl.ds(pl.multiple_of(i * nodes, 16), nodes)]

    for d in range(1, NP):
        q = turn(p, d, NP)
        send(node_rows(part, q), node_rows(part_in, p), p_send.at[d], p_recv.at[p], (g, q, f, s))
    hop_b(4)
    hop_d(2)
    hop_d(3)
    hop_b(5)
    hop_c(4)
    total = part[pl.ds(pl.multiple_of(p * nodes, 16), nodes), :].astype(F32)
    mesh_v = mesh[...]
    u = dot(mesh_v, full[2][:width, :])
    for d in range(1, NP):
        q = turn(p, d, NP)
        got(node_rows(part_in, q), p_recv.at[q])
        total = total + part_in[pl.ds(pl.multiple_of(q * nodes, 16), nodes), :].astype(F32)
    u = u + dot(total.astype(BF), full[2][width:, :])
    mid = (mesh_v.astype(F32) + layer_norm(dot(silu(u), full[3][...]))).astype(BF)
    mine = pl.multiple_of((lane + 1) * nodes, 16)
    ext[pl.ds(mine, nodes), :] = mid
    src = node_rows(ext, lane + 1)
    k = 0
    for df in range(F):
        for ds in range(S):
            if df or ds:
                send(src, src, m_send.at[k], m_recv.at[lane + 1], (g, p, turn(f, df, F), turn(s, ds, S)))
            k += 1

    edge_ends = []
    for want, d, place in ((L - 1, 1, 0), (0, NP - 1, L + 1)):
        copies = []
        k = 0
        for df in range(F):
            for ds in range(S):
                copies.append(
                    pltpu.make_async_remote_copy(
                        src_ref=src, dst_ref=node_rows(ext, place),
                        send_sem=n_send.at[min(place, 1), k], recv_sem=m_recv.at[place],
                        device_id=(g, turn(p, d, NP), df, ds), device_id_type=MESH,
                    )
                )
                k += 1
        edge_ends.append((want, copies))

        @pl.when(lane == want)
        def _():
            for c in copies:
                c.start()

    hop_b(6)
    hop_c(5)
    hop_d(4)
    local[1].wait()
    edge_v = edge[...]
    recv_row = receivers[...]
    recv_hot = one_hot(nodes, 0, recv_row)
    u = dot(edge_v, full[4][:width, :])
    u = u + dot(dot_t(recv_hot, mid).astype(BF), full[4][2 * width:, :])
    hop_b(7)
    hop_c(6)
    hop_d(5)
    for i in range(L + 2):
        @pl.when(lane + 1 != i)
        def _():
            got(node_rows(ext, i), m_recv.at[i])
    send_hot = one_hot((L + 2) * nodes, 0, senders[...])
    u = u + dot(dot_t(send_hot, ext[...]).astype(BF), full[4][width:2 * width, :])
    h = silu(u)
    edge_new = (edge_v.astype(F32) + layer_norm(dot(h, full[5][...]))).astype(BF)
    edge_sum = dot(recv_hot, edge_new).astype(BF)
    hop_b(8)
    hop_c(7)
    hop_d(6)
    hop_d(7)
    u = dot(mid, full[6][:width, :]) + dot(edge_sum, full[6][width:, :])
    h = silu(u)
    mesh_out = (mid.astype(F32) + layer_norm(dot(h, full[7][...]))).astype(BF)
    lane_p[pl.ds(pl.multiple_of(p * nodes, 16), nodes), :] = mesh_out
    for d in range(1, NP):
        send(node_rows(lane_p, p), node_rows(lane_p, p), o_send.at[d], o_recv.at[p], (g, turn(p, d, NP), f, s))
    hop_b(9)
    hop_c(8)
    hop_d(8)
    for c in range(n_chunks):
        at = pl.ds(c * chunk, chunk)
        ahead[at, :] = dot(grid[at, :], full[8][:width, :])
    hop_c(9)
    hop_d(9)
    for d in range(1, NP):
        q = turn(p, d, NP)
        got(node_rows(lane_p, q), o_recv.at[q])

    leave = []

    lane_part = dot(lane_p[...], full[8][width:, :]).astype(BF)
    for c in range(n_chunks):
        at = pl.ds(c * chunk, chunk)
        hot = one_hot(NP * nodes, 0, dec_row[:, c * chunk:(c + 1) * chunk])
        h = silu(ahead[at, :] + dot_t(hot, lane_part))
        res = grid[at, :].astype(F32) + layer_norm(dot(h, full[9][...]))
        outs[at, :] = res.astype(BF)
        copy = pltpu.make_async_copy(outs.at[at], out_h.at[at], out_sem.at[c])
        copy.start()
        leave.append(copy)

    for c in sent:
        c.wait_send()
    for want, copies in edge_ends:
        @pl.when(lane == want)
        def _():
            for c in copies:
                c.wait_send()
    for c in leave:
        c.wait()


def per_device(
    sizes, grid_feat, block_owner, enc_node, dec_node, mesh_feat, edge_feat, senders, receivers, *weights
):
    G, NP, F, S = sizes
    L = F * S
    rows, width = grid_feat.shape
    nodes = mesh_feat.shape[0]
    n_edges = edge_feat.shape[0]
    n_w = len(weights)
    any_spec = pl.BlockSpec(memory_space=pl.ANY)
    vmem = pl.BlockSpec(memory_space=pltpu.VMEM)
    smem = pl.BlockSpec(memory_space=pltpu.SMEM)
    dma = pltpu.SemaphoreType.DMA
    hops = (S - 1) + (F - 1) * (2 + 2 * (S - 1))
    n_chunks = block_owner.shape[0] // 2
    scratch = [pltpu.VMEM((w.shape[0] * L, w.shape[1]), BF) for w in weights] + [
        pltpu.VMEM((rows, width), BF),
        pltpu.VMEM((n_edges, width), BF),
        pltpu.VMEM((rows, width), BF),
        pltpu.VMEM((rows, width), BF),
        pltpu.VMEM((rows, width), F32),
        pltpu.VMEM((NP * nodes, width), BF),
        pltpu.VMEM((NP * nodes, width), BF),
        pltpu.VMEM(((L + 2) * nodes, width), BF),
        pltpu.VMEM((NP * nodes, width), BF),
        dma((2,)),
        dma((n_w,)),
        dma((n_w, hops)),
        dma((n_w, L, 2)),
        dma((NP,)),
        dma((NP,)),
        dma((L,)),
        dma((2, L)),
        dma((L + 2,)),
        dma((NP,)),
        dma((NP,)),
        dma((n_chunks,)),
        pltpu.SemaphoreType.REGULAR((2,)),
    ]
    return pl.pallas_call(
        functools.partial(kernel, sizes),
        out_shape=jax.ShapeDtypeStruct((rows, width), BF),
        in_specs=[any_spec, smem, vmem, vmem, vmem, any_spec, vmem, vmem] + [any_spec] * n_w,
        out_specs=any_spec,
        scratch_shapes=scratch,
        compiler_params=pltpu.CompilerParams(
            collective_id=0, has_side_effects=True, vmem_limit_bytes=56 * 1024 * 1024
        ),
    )(
        grid_feat, block_owner, enc_node.reshape(1, -1), dec_node.reshape(1, -1), mesh_feat, edge_feat,
        senders.reshape(1, -1), receivers.reshape(1, -1), *weights
    )


def solution(mesh):
    every = ("groups", "patch", "feat", "sub")
    sizes = tuple(mesh.shape[a] for a in every)
    row, vec, weight = P(every, None), P(every), P(("feat", "sub"), None)
    in_specs = (row, vec, vec, vec, row, row, vec, vec) + (weight,) * 10
    return jax.shard_map(
        functools.partial(per_device, sizes), mesh=mesh, in_specs=in_specs, out_specs=row, check_vma=False
    )
```

```python
import functools

import jax
import jax.numpy as jnp
from jax import lax
from jax.experimental import pallas as pl
from jax.experimental.pallas import tpu as pltpu
from jax.sharding import PartitionSpec as P

MESH = pl.DeviceIdType.MESH
BF = jnp.bfloat16
F32 = jnp.float32


def dot(a, b):
    return jnp.dot(a, b, preferred_element_type=F32)


def dot_t(a, b):
    return lax.dot_general(a, b, (((0,), (0,)), ((), ())), preferred_element_type=F32)


def silu(u):
    half = 0.5 * u
    return (half + half * jnp.tanh(half)).astype(BF)


def layer_norm(values):
    centred = values - jnp.mean(values, axis=-1, keepdims=True)
    spread = jnp.mean(centred * centred, axis=-1, keepdims=True)
    return centred * lax.rsqrt(spread + 1e-05)


def kernel(sizes, *refs):
    G, NP, F, S = sizes
    L = F * S
    grid_h, owner, enc_node, dec_node, mesh, edge_h, senders, receivers = refs[:8]
    shards = refs[8:18]
    out_h = refs[18]
    full = refs[19:29]
    (
        grid, edge, msgs, outs, ahead, part, part_in, ext, lane_p,
        loc_sem, own_sem, w_send, w_recv, p_send, p_recv, m_send, n_send, m_recv, o_send, o_recv, out_sem, relay_sem,
    ) = refs[29:]
    g, p, f, s = (lax.axis_index(a) for a in ("groups", "patch", "feat", "sub"))
    lane = f * S + s
    n_w = len(shards)
    rows, width = grid.shape
    nodes = mesh.shape[0]
    n_edges = edge.shape[0]
    blocks = owner.shape[0]
    blk = rows // blocks
    chunk = 2 * blk
    n_chunks = rows // chunk
    sent = []

    def turn(i, d, n):
        return lax.rem(i + d, n)

    def send(src, dst, ssem, rsem, dev):
        c = pltpu.make_async_remote_copy(
            src_ref=src, dst_ref=dst, send_sem=ssem, recv_sem=rsem, device_id=dev, device_id_type=MESH
        )
        c.start()
        sent.append(c)

    def got(dst, sem):
        pltpu.make_async_copy(dst, dst, sem).wait()

    local = [pltpu.make_async_copy(grid_h, grid, loc_sem.at[0]), pltpu.make_async_copy(edge_h, edge, loc_sem.at[1])]
    for c in local:
        c.start()

    pairs = ([(g, (1 - g, p, f, s))] if G == 2 else []) + (
        [(lax.rem(p, 2), (g, p + 1 - 2 * lax.rem(p, 2), f, s))] if NP % 2 == 0 else []
    )
    cuts = 2 if pairs else 1

    def half_of(i):
        return pairs[i % len(pairs)][0] if pairs else 0

    def rows_of(i, ln, h=None):
        r = shards[i].shape[0]
        if h is None:
            return full[i].at[pl.ds(pl.multiple_of(ln * r, 16), r)]
        return full[i].at[pl.ds(pl.multiple_of(ln * r + h * (r // cuts), 16), r // cuts)]

    own = [pltpu.make_async_copy(shards[i], rows_of(i, lane), own_sem.at[i]) for i in range(n_w)]
    for c in own:
        c.start()

    barrier = pltpu.get_barrier_semaphore()
    near = [(turn(g, d, G), p, f, s) for d in range(1, G)]
    near += [(g, p, turn(f, df, F), turn(s, ds, S)) for df in range(F) for ds in range(S) if df or ds]
    line = ((p < NP - 1, (g, lax.min(p + 1, NP - 1), f, s)), (p > 0, (g, lax.max(p - 1, 0), f, s)))
    for dev in near:
        pl.semaphore_signal(barrier, inc=1, device_id=dev, device_id_type=MESH)
    for there, dev in line:
        @pl.when(there)
        def _():
            pl.semaphore_signal(barrier, inc=1, device_id=dev, device_id_type=MESH)
    pl.semaphore_wait(barrier, len(near) + sum(there.astype(jnp.int32) for there, _ in line))

    def relay():
        for k in range(2):
            (there, dev), (back, _) = line[k], line[1 - k]

            @pl.when(back)
            def _():
                pl.semaphore_wait(relay_sem.at[k], 1)

            @pl.when(there)
            def _():
                pl.semaphore_signal(relay_sem.at[k], inc=1, device_id=dev, device_id_type=MESH)

    slot = [0] * n_w

    def w_out(i, src, dst, rsem, dev):
        send(src, dst, w_send.at[i, slot[i]], rsem, dev)
        slot[i] += 1

    def hop_a(i):
        r = shards[i].shape[0] // cuts
        h = half_of(i)
        for df in range(1, F):
            src = shards[i].at[pl.ds(pl.multiple_of(h * r, 16), r)]
            w_out(i, src, rows_of(i, lane, h), w_recv.at[i, lane, h], (g, p, turn(f, df, F), s))
        for ds in range(1, S):
            w_out(i, shards[i], rows_of(i, lane), w_recv.at[i, lane, 0], (g, p, f, turn(s, ds, S)))

    def hop_b(i):
        h = half_of(i)
        for df in range(1, F):
            ln = turn(f, df, F) * S + s
            buf, sem = rows_of(i, ln, h), w_recv.at[i, ln, h]
            got(buf, sem)
            if pairs:
                w_out(i, buf, buf, sem, pairs[i % len(pairs)][1])
            for ds in range(1, S):
                w_out(i, buf, buf, sem, (g, p, f, turn(s, ds, S)))

    def hop_c(i):
        if not pairs:
            return
        h = 1 - half_of(i)
        for df in range(1, F):
            ln = turn(f, df, F) * S + s
            buf, sem = rows_of(i, ln, h), w_recv.at[i, ln, h]
            got(buf, sem)
            for ds in range(1, S):
                w_out(i, buf, buf, sem, (g, p, f, turn(s, ds, S)))

    def hop_d(i):
        own[i].wait()
        for ds in range(1, S):
            so = turn(s, ds, S)
            got(rows_of(i, f * S + so), w_recv.at[i, f * S + so, 0])
            for df in range(1, F):
                ln = turn(f, df, F) * S + so
                for h in range(cuts):
                    got(rows_of(i, ln, h), w_recv.at[i, ln, h])

    for i in range(n_w):
        hop_a(i)
    relay()
    hop_b(0)
    hop_b(1)
    hop_c(0)
    hop_b(2)
    hop_c(1)
    hop_d(0)
    hop_d(1)
    local[0].wait()

    between = {n_chunks // 2 - 1: [lambda: hop_b(3), lambda: hop_c(2)], n_chunks - 1: [lambda: hop_c(3), lambda: hop_b(4)]}
    for c in range(n_chunks):
        at = pl.ds(c * chunk, chunk)
        h = silu(dot(grid[at, :], full[0][...]))
        msgs[at, :] = layer_norm(dot(h, full[1][...])).astype(BF)
        for step in between.get(c, []):
            step()

    def one_hot(count, first, row):
        ids = lax.broadcasted_iota(jnp.int32, (count, row.shape[1]), 0) + first
        return jnp.where(ids == row, 1.0, 0.0).astype(BF)

    enc_row = jnp.concatenate(
        [enc_node[:, b * blk:(b + 1) * blk] + owner[b] * nodes for b in range(blocks)], axis=1
    )
    dec_row = jnp.concatenate(
        [dec_node[:, b * blk:(b + 1) * blk] + owner[b] * nodes for b in range(blocks)], axis=1
    )
    some = min(NP, 4)
    for q in range(0, NP, some):
        total = dot(one_hot(some * nodes, q * nodes, enc_row), msgs[...])
        part[q * nodes:(q + some) * nodes, :] = total.astype(BF)

    def node_rows(ref, i):
        return ref.at[pl.ds(pl.multiple_of(i * nodes, 16), nodes)]

    for d in range(1, NP):
        q = turn(p, d, NP)
        send(node_rows(part, q), node_rows(part_in, p), p_send.at[d], p_recv.at[p], (g, q, f, s))
    hop_d(2)
    hop_d(3)
    hop_b(5)
    hop_c(4)
    hop_b(6)
    total = part[pl.ds(pl.multiple_of(p * nodes, 16), nodes), :].astype(F32)
    mesh_v = mesh[...]
    u = dot(mesh_v, full[2][:width, :])
    for d in range(1, NP):
        q = turn(p, d, NP)
        got(node_rows(part_in, q), p_recv.at[q])
        total = total + part_in[pl.ds(pl.multiple_of(q * nodes, 16), nodes), :].astype(F32)
    u = u + dot(total.astype(BF), full[2][width:, :])
    mid = (mesh_v.astype(F32) + layer_norm(dot(silu(u), full[3][...]))).astype(BF)
    mine = pl.multiple_of((lane + 1) * nodes, 16)
    ext[pl.ds(mine, nodes), :] = mid
    src = node_rows(ext, lane + 1)
    k = 0
    for df in range(F):
        for ds in range(S):
            if df or ds:
                send(src, src, m_send.at[k], m_recv.at[lane + 1], (g, p, turn(f, df, F), turn(s, ds, S)))
            k += 1

    edge_ends = []
    for want, d, place in ((L - 1, 1, 0), (0, NP - 1, L + 1)):
        copies = []
        k = 0
        for df in range(F):
            for ds in range(S):
                copies.append(
                    pltpu.make_async_remote_copy(
                        src_ref=src, dst_ref=node_rows(ext, place),
                        send_sem=n_send.at[min(place, 1), k], recv_sem=m_recv.at[place],
                        device_id=(g, turn(p, d, NP), df, ds), device_id_type=MESH,
                    )
                )
                k += 1
        edge_ends.append((want, copies))

        @pl.when(lane == want)
        def _():
            for c in copies:
                c.start()

    hop_c(5)
    hop_b(7)
    hop_d(4)
    local[1].wait()
    edge_v = edge[...]
    recv_row = receivers[...]
    recv_hot = one_hot(nodes, 0, recv_row)
    u = dot(edge_v, full[4][:width, :])
    u = u + dot(dot_t(recv_hot, mid).astype(BF), full[4][2 * width:, :])
    hop_c(6)
    hop_d(5)
    hop_b(8)
    for i in range(L + 2):
        @pl.when(lane + 1 != i)
        def _():
            got(node_rows(ext, i), m_recv.at[i])
    send_hot = one_hot((L + 2) * nodes, 0, senders[...])
    u = u + dot(dot_t(send_hot, ext[...]).astype(BF), full[4][width:2 * width, :])
    h = silu(u)
    edge_new = (edge_v.astype(F32) + layer_norm(dot(h, full[5][...]))).astype(BF)
    edge_sum = dot(recv_hot, edge_new).astype(BF)
    hop_c(7)
    hop_b(9)
    hop_c(8)
    hop_d(6)
    hop_d(7)
    u = dot(mid, full[6][:width, :]) + dot(edge_sum, full[6][width:, :])
    h = silu(u)
    mesh_out = (mid.astype(F32) + layer_norm(dot(h, full[7][...]))).astype(BF)
    lane_p[pl.ds(pl.multiple_of(p * nodes, 16), nodes), :] = mesh_out
    for d in range(1, NP):
        send(node_rows(lane_p, p), node_rows(lane_p, p), o_send.at[d], o_recv.at[p], (g, turn(p, d, NP), f, s))
    hop_c(9)
    hop_d(8)
    for c in range(n_chunks):
        at = pl.ds(c * chunk, chunk)
        ahead[at, :] = dot(grid[at, :], full[8][:width, :])
    hop_d(9)
    for d in range(1, NP):
        q = turn(p, d, NP)
        got(node_rows(lane_p, q), o_recv.at[q])

    leave = []

    lane_part = dot(lane_p[...], full[8][width:, :]).astype(BF)
    for c in range(n_chunks):
        at = pl.ds(c * chunk, chunk)
        hot = one_hot(NP * nodes, 0, dec_row[:, c * chunk:(c + 1) * chunk])
        h = silu(ahead[at, :] + dot_t(hot, lane_part))
        res = grid[at, :].astype(F32) + layer_norm(dot(h, full[9][...]))
        outs[at, :] = res.astype(BF)
        copy = pltpu.make_async_copy(outs.at[at], out_h.at[at], out_sem.at[c])
        copy.start()
        leave.append(copy)

    for c in sent:
        c.wait_send()
    for want, copies in edge_ends:
        @pl.when(lane == want)
        def _():
            for c in copies:
                c.wait_send()
    for c in leave:
        c.wait()


def per_device(
    sizes, grid_feat, block_owner, enc_node, dec_node, mesh_feat, edge_feat, senders, receivers, *weights
):
    G, NP, F, S = sizes
    L = F * S
    rows, width = grid_feat.shape
    nodes = mesh_feat.shape[0]
    n_edges = edge_feat.shape[0]
    n_w = len(weights)
    any_spec = pl.BlockSpec(memory_space=pl.ANY)
    vmem = pl.BlockSpec(memory_space=pltpu.VMEM)
    smem = pl.BlockSpec(memory_space=pltpu.SMEM)
    dma = pltpu.SemaphoreType.DMA
    hops = (S - 1) + (F - 1) * (2 + 2 * (S - 1))
    n_chunks = block_owner.shape[0] // 2
    scratch = [pltpu.VMEM((w.shape[0] * L, w.shape[1]), BF) for w in weights] + [
        pltpu.VMEM((rows, width), BF),
        pltpu.VMEM((n_edges, width), BF),
        pltpu.VMEM((rows, width), BF),
        pltpu.VMEM((rows, width), BF),
        pltpu.VMEM((rows, width), F32),
        pltpu.VMEM((NP * nodes, width), BF),
        pltpu.VMEM((NP * nodes, width), BF),
        pltpu.VMEM(((L + 2) * nodes, width), BF),
        pltpu.VMEM((NP * nodes, width), BF),
        dma((2,)),
        dma((n_w,)),
        dma((n_w, hops)),
        dma((n_w, L, 2)),
        dma((NP,)),
        dma((NP,)),
        dma((L,)),
        dma((2, L)),
        dma((L + 2,)),
        dma((NP,)),
        dma((NP,)),
        dma((n_chunks,)),
        pltpu.SemaphoreType.REGULAR((2,)),
    ]
    return pl.pallas_call(
        functools.partial(kernel, sizes),
        out_shape=jax.ShapeDtypeStruct((rows, width), BF),
        in_specs=[any_spec, smem, vmem, vmem, vmem, any_spec, vmem, vmem] + [any_spec] * n_w,
        out_specs=any_spec,
        scratch_shapes=scratch,
        compiler_params=pltpu.CompilerParams(
            collective_id=0, has_side_effects=True, vmem_limit_bytes=56 * 1024 * 1024
        ),
    )(
        grid_feat, block_owner, enc_node.reshape(1, -1), dec_node.reshape(1, -1), mesh_feat, edge_feat,
        senders.reshape(1, -1), receivers.reshape(1, -1), *weights
    )


def solution(mesh):
    every = ("groups", "patch", "feat", "sub")
    sizes = tuple(mesh.shape[a] for a in every)
    row, vec, weight = P(every, None), P(every), P(("feat", "sub"), None)
    in_specs = (row, vec, vec, vec, row, row, vec, vec) + (weight,) * 10
    return jax.shard_map(
        functools.partial(per_device, sizes), mesh=mesh, in_specs=in_specs, out_specs=row, check_vma=False
    )
```
